32 devices in a mesh: ctx: 16 (over z, y, core), head: 2 (over x).
Axes of the slice: x: 2, y: 2, z: 4, core: 2. Of those that a mesh axis runs over, the one named last changes fastest.
Arguments:
- queries: bfloat16 [2048, 8192], P('ctx', 'head'), may hold values from -5 to 5
- key_rows: bfloat16 [2048, 1024], P('ctx', 'head'), may hold values from -5 to 5
- value_rows: bfloat16 [2048, 1024], P('ctx', 'head'), may hold values from -6 to 6
- query_tangent: bfloat16 [2048, 8192], P('ctx', 'head'), may hold values from -16 to 16
- key_tangent: bfloat16 [2048, 1024], P('ctx', 'head'), may hold values from -3 to 3
- value_tangent: bfloat16 [2048, 1024], P('ctx', 'head'), may hold values from -6 to 6
- block_order: int32 [16], replicated, may hold values from 0 to 15, each once
Outputs:
- attended: bfloat16 [2048, 8192], P('ctx', 'head')
- probe_out: bfloat16 [2048, 8192], P('ctx', 'head')
- probe_norm: float32 [], replicated
The draws below stay inside these ranges and needn't reach their ends.
Inputs may be any that keep to these rules, and one draw needn't show every extreme that they name: `block_order`: each block index appears exactly once.
All inputs are finite; a program needn't handle non-finite values.
Results may differ from the reference program's by a relative error of at most 0.025.
Values may be sent and summed in bfloat16 or wider, within the bound.
A program may use at most 64 MiB of HBM per device.

```python
import math
import jax
import jax.numpy as jnp
from jax import lax

Q_HEADS = 64
KV_HEADS = 8
HEAD_DIM = 128
TOK_DEV = 128
SEQUENCE = 2048
N_CTX = 16


def paired_rows(key):
    base = jax.random.fold_in(key, 11)
    key_q, key_k = jax.random.split(base, 2)
    width_q = Q_HEADS * HEAD_DIM
    width_k = KV_HEADS * HEAD_DIM
    query_part = jnp.clip(1.6 * jax.random.normal(key_q, (SEQUENCE, width_q)), -5.0, 5.0)
    key_part = jnp.clip(1.6 * jax.random.normal(key_k, (SEQUENCE, width_k)), -5.0, 5.0)
    return (query_part, key_part)


def draw_queries(key, part):
    query_part, key_part = paired_rows(key)
    return query_part.astype(jnp.bfloat16)


def draw_key_rows(key, part):
    query_part, key_part = paired_rows(key)
    return key_part.astype(jnp.bfloat16)


def draw_query_tangent(key, part):
    base = jax.random.fold_in(key, 23)
    key_raw, key_spread = jax.random.split(base, 2)
    width_q = Q_HEADS * HEAD_DIM
    fraction = jnp.arange(SEQUENCE, dtype=jnp.float32) / max(SEQUENCE - 1, 1)
    spread = jax.random.uniform(key_spread, (SEQUENCE,))
    row_scale = 10.0 ** (0.5 * fraction + 0.5 * spread)
    raw = jnp.clip(0.4 * jax.random.normal(key_raw, (SEQUENCE, width_q)), -1.6, 1.6)
    return (raw * row_scale[:, None]).astype(jnp.bfloat16)


def block_scale(key, dims, cuts, smallest, high):
    def one(dim, shards_of):
        heights = jax.random.uniform(jax.random.fold_in(jax.random.fold_in(key, 6), dim), (shards_of,), jnp.float32, smallest / len(cuts), high / len(cuts))
        return jnp.repeat(jnp.exp(heights), dims[dim] // shards_of).reshape((-1,) + (1,) * (len(dims) - dim - 1))

    loudness = one(*cuts[0])
    for cut in cuts[1:]:
        loudness = loudness * one(*cut)
    return loudness


def bell_draw(key, dims, deviation, reach, pieces=(), kind=jnp.bfloat16):
    values = jax.random.normal(key, dims, jnp.float32) * deviation
    if len(pieces) > 0:
        values = block_scale(key, dims, pieces, -0.22, 0.18) * values
    return jnp.clip(values, min=-reach, max=reach).astype(kind)


def setup_inputs(seed: int = 0) -> dict:
    key_list = jax.random.split(jax.random.key(seed), 8)
    return {
        "queries": draw_queries(jax.random.fold_in(key_list[7], 71), 0),
        "key_rows": draw_key_rows(jax.random.fold_in(key_list[7], 71), 0),
        "value_rows": bell_draw(key_list[2], (SEQUENCE, KV_HEADS * HEAD_DIM), 1.0, 6.0, ((0, 16), (1, 2))),
        "query_tangent": draw_query_tangent(jax.random.fold_in(key_list[7], 71), 0),
        "key_tangent": bell_draw(key_list[4], (SEQUENCE, KV_HEADS * HEAD_DIM), 0.5, 3.0, ((0, 16), (1, 2))),
        "value_tangent": bell_draw(key_list[5], (SEQUENCE, KV_HEADS * HEAD_DIM), 1.0, 6.0, ((0, 16), (1, 2))),
        "block_order": jax.random.permutation(key_list[6], N_CTX).astype(jnp.int32),
    }


floor_score = -1e+30

def reference(queries, key_rows, value_rows, query_tangent, key_tangent, value_tangent, block_order):
    row_index = jnp.arange(SEQUENCE, dtype=jnp.int32)
    position = block_order[row_index // TOK_DEV].astype(jnp.int32) * TOK_DEV + row_index % TOK_DEV
    visible = position[None, :] <= position[:, None]
    shares = Q_HEADS // KV_HEADS
    factor = 1.0 / math.sqrt(HEAD_DIM)

    def per_head(head):
        group = head // shares
        q_head = lax.dynamic_slice_in_dim(queries, head * HEAD_DIM, HEAD_DIM, 1)
        dq_head = lax.dynamic_slice_in_dim(query_tangent, head * HEAD_DIM, HEAD_DIM, 1)
        k_head = lax.dynamic_slice_in_dim(key_rows, group * HEAD_DIM, HEAD_DIM, 1)
        dk_head = lax.dynamic_slice_in_dim(key_tangent, group * HEAD_DIM, HEAD_DIM, 1)
        v_head = lax.dynamic_slice_in_dim(value_rows, group * HEAD_DIM, HEAD_DIM, 1)
        dv_head = lax.dynamic_slice_in_dim(value_tangent, group * HEAD_DIM, HEAD_DIM, 1)
        scores = jnp.dot(q_head, k_head.T, preferred_element_type=jnp.float32) * factor
        masked = jnp.where(visible, scores, floor_score)
        top = lax.optimization_barrier(jnp.max(masked, axis=1, keepdims=True))
        weights = jnp.where(visible, jnp.exp(masked - top), 0.0)
        totals = lax.optimization_barrier(jnp.sum(weights, axis=1, keepdims=True))
        slopes = (jnp.dot(dq_head, k_head.T, preferred_element_type=jnp.float32) + jnp.dot(q_head, dk_head.T, preferred_element_type=jnp.float32)) * factor
        tilted = weights * slopes
        drifts = lax.optimization_barrier(jnp.sum(tilted, axis=1, keepdims=True))
        low_weights = weights.astype(jnp.bfloat16)
        low_tilted = tilted.astype(jnp.bfloat16)
        numerator = jnp.dot(low_weights, v_head, preferred_element_type=jnp.float32)
        tangent_num = jnp.dot(low_tilted, v_head, preferred_element_type=jnp.float32) + jnp.dot(low_weights, dv_head, preferred_element_type=jnp.float32)
        attended = (numerator / totals).astype(jnp.bfloat16)
        probe = (tangent_num - numerator * drifts / totals) / totals
        return (attended, probe)
    heads_out, probes = lax.map(per_head, jnp.arange(Q_HEADS, dtype=jnp.int32))
    attended = heads_out.transpose(1, 0, 2).reshape(SEQUENCE, Q_HEADS * HEAD_DIM)
    probe_all = probes.transpose(1, 0, 2).reshape(SEQUENCE, Q_HEADS * HEAD_DIM)
    probe_norm = jnp.sqrt(jnp.sum(probe_all * probe_all) / (SEQUENCE * Q_HEADS * HEAD_DIM))
    return (attended, probe_all.astype(jnp.bfloat16), probe_norm)
```

```python
import functools
import math

import jax
import jax.numpy as jnp
from jax import lax
from jax.experimental import pallas as pl
from jax.experimental.pallas import tpu as pltpu
from jax.sharding import PartitionSpec as P

HEAD_DIM = 128
MESH = pl.DeviceIdType.MESH
FLOOR = -1e30


def dot_t(a, b):
    return lax.dot_general(a, b, (((1,), (1,)), ((), ())), preferred_element_type=jnp.float32)


def dot_n(a, b):
    return jnp.dot(a, b, preferred_element_type=jnp.float32)


def kernel(
    n,
    order_ref, q_hbm, dq_hbm, k_ref, v_ref, dk_ref, dv_ref,
    att_ref, probe_ref, square_ref,
    q_vm, dq_vm, qs, kv, acc, tan, top, tot, dri,
    q_sem, recv, send,
):
    depth = n // 4
    me = lax.axis_index("ctx")
    z, y, c = me // 4, (me // 2) % 2, me % 2
    rows = k_ref.shape[0]
    groups = k_ref.shape[1] // HEAD_DIM
    shares = q_vm.shape[1] // k_ref.shape[1]
    stack = rows * shares
    steps = depth * groups

    def at(zz, yy, cc):
        return {"ctx": (zz * 2 + yy) * 2 + cc}

    copies = [
        pltpu.make_async_copy(q_hbm, q_vm, q_sem.at[0]),
        pltpu.make_async_copy(dq_hbm, dq_vm, q_sem.at[1]),
    ]
    for copy in copies:
        copy.start()

    barrier = pltpu.get_barrier_semaphore()
    has_up, has_down = z < depth - 1, z > 0

    def greet(zz, yy, cc):
        pl.semaphore_signal(barrier, inc=1, device_id=at(zz, yy, cc), device_id_type=MESH)

    greet(z, 1 - y, c)
    greet(z, y, 1 - c)

    @pl.when(has_up)
    def _():
        greet(z + 1, y, c)

    @pl.when(has_down)
    def _():
        greet(z - 1, y, c)

    for g in range(groups):
        cols = slice(g * HEAD_DIM, (g + 1) * HEAD_DIM)
        for part, ref in enumerate((k_ref, dk_ref, v_ref, dv_ref)):
            kv[z, g, y, c, :, part * HEAD_DIM : (part + 1) * HEAD_DIM] = ref[:, cols]

    peers = 2 + jnp.where(has_up, 1, 0) + jnp.where(has_down, 1, 0)
    pl.semaphore_wait(barrier, peers)

    def move(zs, g, yy, cc, lane, target):
        return pltpu.make_async_remote_copy(
            src_ref=kv.at[zs, g, yy, cc],
            dst_ref=kv.at[zs, g, yy, cc],
            send_sem=send.at[zs, g, lane],
            recv_sem=recv.at[zs, g, yy, cc],
            device_id=target,
            device_id_type=MESH,
        )

    def up(zs, g):
        return move(zs, g, y, c, 0, at(z + 1, y, c))

    def down(zs, g):
        return move(zs, g, y, c, 1, at(z - 1, y, c))

    def across(zs, g):
        return move(zs, g, y, c, 2, at(z, 1 - y, c))

    def twin(zs, g):
        return move(zs, g, y, c, 3, at(z, y, 1 - c))

    def twin_across(zs, g):
        return move(zs, g, 1 - y, c, 4, at(z, y, 1 - c))

    def goes_up(zs):
        return jnp.logical_and(has_up, zs <= z)

    def goes_down(zs):
        return jnp.logical_and(has_down, zs >= z)

    def pass_on(zs, g):
        @pl.when(goes_up(zs))
        def _():
            up(zs, g).start()

        @pl.when(goes_down(zs))
        def _():
            down(zs, g).start()

        across(zs, g).start()
        twin(zs, g).start()

    for g in range(groups):
        pass_on(z, g)

    for copy in copies:
        copy.wait()

    def stage(g, carry):
        for h in range(shares):
            cols = pl.ds(pl.multiple_of((g * shares + h) * HEAD_DIM, HEAD_DIM), HEAD_DIM)
            qs[g, h * rows : (h + 1) * rows, 0:HEAD_DIM] = dq_vm[:, cols]
            qs[g, h * rows : (h + 1) * rows, HEAD_DIM:] = q_vm[:, cols]
        return carry

    lax.fori_loop(0, groups, stage, 0)

    reach = jnp.minimum(z, depth - 1 - z)
    far = jnp.where(z < depth - 1 - z, 1, -1)

    def source(i):
        near = ((i + 1) // 2) * jnp.where(i % 2 == 1, 1, -1)
        return z + jnp.where(i <= 2 * reach, near, (i - reach) * far)

    own = order_ref[me]
    factor = 1.0 / math.sqrt(HEAD_DIM)
    sharp = factor * math.log2(math.e)
    part_rows = min(stack, 512)

    def fold(zs, g, first):
        block = kv[zs, g].reshape(4 * rows, 4 * HEAD_DIM)
        orders = [order_ref[zs * 4 + j] for j in range(4)]
        if first:
            lane = lax.broadcasted_iota(jnp.int32, (part_rows, rows), 1)
            row = lax.broadcasted_iota(jnp.int32, (part_rows, rows), 0) % rows + own * rows

        def part(r, carry):
            span = pl.ds(pl.multiple_of(r * part_rows, part_rows), part_rows)
            pair = qs[g, span, :]
            scores = dot_t(pair[:, HEAD_DIM:], block[:, :HEAD_DIM]) * sharp
            slopes = dot_t(pair, block[:, : 2 * HEAD_DIM])
            pieces = []
            for j in range(4):
                piece = scores[:, j * rows : (j + 1) * rows]
                if first:
                    piece = jnp.where(lane + orders[j] * rows <= row, piece, FLOOR)
                else:
                    piece = piece + jnp.where(orders[j] <= own, 0.0, FLOOR)
                pieces.append(piece)
            high = jnp.maximum(
                jnp.maximum(pieces[0], pieces[1]), jnp.maximum(pieces[2], pieces[3])
            )
            high = jnp.broadcast_to(jnp.max(high, axis=1, keepdims=True), high.shape)
            if not first:
                old = top[g, span, :]
                high = jnp.maximum(old, high)
                shrink = jnp.exp2(old - high)
            top[g, span, :] = high
            weights, tilted = [], []
            for j in range(4):
                weights.append(jnp.exp2(pieces[j] - high))
                tilted.append(weights[j] * slopes[:, j * rows : (j + 1) * rows])
            tot_new = (weights[0] + weights[1]) + (weights[2] + weights[3])
            dri_new = (tilted[0] + tilted[1]) + (tilted[2] + tilted[3])
            low_w = jnp.concatenate([w.astype(jnp.bfloat16) for w in weights], axis=1)
            low_t = jnp.concatenate([t.astype(jnp.bfloat16) for t in tilted], axis=1)
            acc_new = dot_n(low_w, block[:, 2 * HEAD_DIM :])
            tan_new = dot_n(low_t, block[:, 2 * HEAD_DIM : 3 * HEAD_DIM])
            if first:
                tot[g, span, :] = tot_new
                dri[g, span, :] = dri_new
                acc[g, span, :] = acc_new
                tan[g, span, :] = tan_new
            else:
                tot[g, span, :] = tot[g, span, :] * shrink + tot_new
                dri[g, span, :] = dri[g, span, :] * shrink + dri_new
                tan[g, span, :] = tan[g, span, :] * shrink + tan_new
                acc[g, span, :] = (
                    acc[g, span, :] * jnp.concatenate([shrink, shrink], axis=1) + acc_new
                )
            return carry

        lax.fori_loop(0, stack // part_rows, part, 0)

    def turn(s, carry):
        @pl.when(jnp.logical_and(s >= groups, s < steps))
        def _():
            zs, g = source(s // groups), s % groups
            twin(zs, g).wait_recv()
            pass_on(zs, g)

        @pl.when(jnp.logical_and(s >= 1, s < steps + 1))
        def _():
            zs, g = source((s - 1) // groups), (s - 1) % groups
            twin_across(zs, g).wait_recv()
            twin_across(zs, g).start()

        def ready(zs, g):
            move(zs, g, y, 1 - c, 0, at(z, y, 1 - c)).wait_recv()
            move(zs, g, 1 - y, 1 - c, 0, at(z, y, 1 - c)).wait_recv()

        @pl.when(jnp.logical_and(s >= 2, s < groups + 2))
        def _():
            g = s - 2
            ready(z, g)
            fold(z, g, True)

        @pl.when(s >= groups + 2)
        def _():
            zs, g = source((s - 2) // groups), (s - 2) % groups
            ready(zs, g)
            fold(zs, g, False)

        return carry

    lax.fori_loop(0, steps + 2, turn, 0)

    def finish(g, squares):
        for h in range(shares):
            span = slice(h * rows, (h + 1) * rows)
            cols = pl.ds(pl.multiple_of((g * shares + h) * HEAD_DIM, HEAD_DIM), HEAD_DIM)
            inverse = 1.0 / jnp.sum(tot[g, span, :], axis=1, keepdims=True)
            drift = jnp.sum(dri[g, span, :], axis=1, keepdims=True) * factor
            numer = acc[g, span, :HEAD_DIM] * inverse
            tangent = (tan[g, span, :] * factor + acc[g, span, HEAD_DIM:]) * inverse
            probe = tangent - numer * (drift * inverse)
            att_ref[:, cols] = numer.astype(jnp.bfloat16)
            probe_ref[:, cols] = probe.astype(jnp.bfloat16)
            squares = squares + jnp.sum((probe * probe).reshape(rows // 8, 8, HEAD_DIM), axis=0)
        return squares

    square_ref[...] = lax.fori_loop(
        0, groups, finish, jnp.zeros((8, HEAD_DIM), jnp.float32)
    )

    def settle(s, carry):
        zs, g = s // groups, s % groups

        @pl.when(goes_up(zs))
        def _():
            up(zs, g).wait_send()

        @pl.when(goes_down(zs))
        def _():
            down(zs, g).wait_send()

        across(zs, g).wait_send()
        twin(zs, g).wait_send()
        twin_across(zs, g).wait_send()
        return carry

    lax.fori_loop(0, steps, settle, 0)


def shards(n, heads, queries, key_rows, value_rows, query_tangent, key_tangent, value_tangent, block_order):
    rows, width = queries.shape
    groups = key_rows.shape[1] // HEAD_DIM
    stack = rows * width // key_rows.shape[1]
    depth = n // 4
    vmem = pl.BlockSpec(memory_space=pltpu.VMEM)
    hbm = pl.BlockSpec(memory_space=pl.ANY)
    f32, bf16 = jnp.float32, jnp.bfloat16
    attended, probe_out, squares = pl.pallas_call(
        functools.partial(kernel, n),
        out_shape=(
            jax.ShapeDtypeStruct((rows, width), bf16),
            jax.ShapeDtypeStruct((rows, width), bf16),
            jax.ShapeDtypeStruct((8, HEAD_DIM), f32),
        ),
        in_specs=[pl.BlockSpec(memory_space=pltpu.SMEM), hbm, hbm, vmem, vmem, vmem, vmem],
        out_specs=(vmem, vmem, vmem),
        scratch_shapes=[
            pltpu.VMEM((rows, width), bf16),
            pltpu.VMEM((rows, width), bf16),
            pltpu.VMEM((groups, stack, 2 * HEAD_DIM), bf16),
            pltpu.VMEM((depth, groups, 2, 2, rows, 4 * HEAD_DIM), bf16),
            pltpu.VMEM((groups, stack, 2 * HEAD_DIM), f32),
            pltpu.VMEM((groups, stack, HEAD_DIM), f32),
            pltpu.VMEM((groups, stack, HEAD_DIM), f32),
            pltpu.VMEM((groups, stack, HEAD_DIM), f32),
            pltpu.VMEM((groups, stack, HEAD_DIM), f32),
            pltpu.SemaphoreType.DMA((2,)),
            pltpu.SemaphoreType.DMA((depth, groups, 2, 2)),
            pltpu.SemaphoreType.DMA((depth, groups, 5)),
        ],
        compiler_params=pltpu.CompilerParams(
            collective_id=0, has_side_effects=True, vmem_limit_bytes=56 * 2**20
        ),
    )(block_order, queries, query_tangent, key_rows, value_rows, key_tangent, value_tangent)
    total_squares = lax.psum(jnp.sum(squares), ("ctx", "head"))
    entries = rows * width * n * heads
    return attended, probe_out, jnp.sqrt(total_squares / entries)


def solution(mesh):
    split = P("ctx", "head")
    return jax.shard_map(
        functools.partial(shards, mesh.shape["ctx"], mesh.shape["head"]),
        mesh=mesh,
        in_specs=(split,) * 6 + (P(),),
        out_specs=(split, split, P()),
        check_vma=False,
    )
```

```python
import functools
import math

import jax
import jax.numpy as jnp
from jax import lax
from jax.experimental import pallas as pl
from jax.experimental.pallas import tpu as pltpu
from jax.sharding import PartitionSpec as P

HEAD_DIM = 128
MESH = pl.DeviceIdType.MESH
FLOOR = -1e30


def dot_t(a, b):
    return lax.dot_general(a, b, (((1,), (1,)), ((), ())), preferred_element_type=jnp.float32)


def dot_n(a, b):
    return jnp.dot(a, b, preferred_element_type=jnp.float32)


def kernel(
    n,
    heads,
    order_ref, q_hbm, dq_hbm, k_ref, v_ref, dk_ref, dv_ref,
    att_ref, probe_ref, norm_ref,
    q_vm, dq_vm, qs, kv, acc, tan, top, tot, dri,
    plane_box, line_box, head_box,
    q_sem, recv, send, plane_sem, line_sem, head_sem,
):
    depth = n // 4
    me = lax.axis_index("ctx")
    z, y, c = me // 4, (me // 2) % 2, me % 2
    rows = k_ref.shape[0]
    groups = k_ref.shape[1] // HEAD_DIM
    shares = q_vm.shape[1] // k_ref.shape[1]
    stack = rows * shares
    steps = depth * groups

    def at(zz, yy, cc):
        return {"ctx": (zz * 2 + yy) * 2 + cc}

    copies = [
        pltpu.make_async_copy(q_hbm, q_vm, q_sem.at[0]),
        pltpu.make_async_copy(dq_hbm, dq_vm, q_sem.at[1]),
    ]
    for copy in copies:
        copy.start()

    barrier = pltpu.get_barrier_semaphore()
    has_up, has_down = z < depth - 1, z > 0

    head = lax.axis_index("head")
    spot = y * 2 + c
    plane = (4, spot, lambda i: {"ctx": z * 4 + i})
    line = (depth, z, lambda i: {"ctx": i * 4 + spot})
    across_heads = (heads, head, lambda i: {"head": i})
    for count, mine, device in (plane, line, across_heads):
        for step in range(1, count):
            pl.semaphore_signal(
                barrier, inc=1, device_id=device((mine + step) % count), device_id_type=MESH
            )

    for g in range(groups):
        cols = slice(g * HEAD_DIM, (g + 1) * HEAD_DIM)
        for part, ref in enumerate((k_ref, dk_ref, v_ref, dv_ref)):
            kv[z, g, y, c, :, part * HEAD_DIM : (part + 1) * HEAD_DIM] = ref[:, cols]

    pl.semaphore_wait(barrier, 3 + (depth - 1) + (heads - 1))

    def move(zs, g, yy, cc, lane, target):
        return pltpu.make_async_remote_copy(
            src_ref=kv.at[zs, g, yy, cc],
            dst_ref=kv.at[zs, g, yy, cc],
            send_sem=send.at[zs, g, lane],
            recv_sem=recv.at[zs, g, yy, cc],
            device_id=target,
            device_id_type=MESH,
        )

    def up(zs, g):
        return move(zs, g, y, c, 0, at(z + 1, y, c))

    def down(zs, g):
        return move(zs, g, y, c, 1, at(z - 1, y, c))

    def across(zs, g):
        return move(zs, g, y, c, 2, at(z, 1 - y, c))

    def twin(zs, g):
        return move(zs, g, y, c, 3, at(z, y, 1 - c))

    def twin_across(zs, g):
        return move(zs, g, 1 - y, c, 4, at(z, y, 1 - c))

    def goes_up(zs):
        return jnp.logical_and(has_up, zs <= z)

    def goes_down(zs):
        return jnp.logical_and(has_down, zs >= z)

    def pass_on(zs, g):
        @pl.when(goes_up(zs))
        def _():
            up(zs, g).start()

        @pl.when(goes_down(zs))
        def _():
            down(zs, g).start()

        across(zs, g).start()
        twin(zs, g).start()

    for g in range(groups):
        pass_on(z, g)

    for copy in copies:
        copy.wait()

    def stage(g, carry):
        for h in range(shares):
            cols = pl.ds(pl.multiple_of((g * shares + h) * HEAD_DIM, HEAD_DIM), HEAD_DIM)
            qs[g, h * rows : (h + 1) * rows, 0:HEAD_DIM] = dq_vm[:, cols]
            qs[g, h * rows : (h + 1) * rows, HEAD_DIM:] = q_vm[:, cols]
        return carry

    lax.fori_loop(0, groups, stage, 0)

    reach = jnp.minimum(z, depth - 1 - z)
    far = jnp.where(z < depth - 1 - z, 1, -1)

    def source(i):
        near = ((i + 1) // 2) * jnp.where(i % 2 == 1, 1, -1)
        return z + jnp.where(i <= 2 * reach, near, (i - reach) * far)

    own = order_ref[me]
    factor = 1.0 / math.sqrt(HEAD_DIM)
    sharp = factor * math.log2(math.e)
    part_rows = min(stack, 1024)

    def fold(zs, g, first):
        block = kv[zs, g].reshape(4 * rows, 4 * HEAD_DIM)
        orders = [order_ref[zs * 4 + j] for j in range(4)]
        if first:
            lane = lax.broadcasted_iota(jnp.int32, (part_rows, rows), 1)
            row = lax.broadcasted_iota(jnp.int32, (part_rows, rows), 0) % rows + own * rows

        def part(r, carry):
            span = pl.ds(pl.multiple_of(r * part_rows, part_rows), part_rows)
            pair = qs[g, span, :]
            scores = dot_t(pair[:, HEAD_DIM:], block[:, :HEAD_DIM]) * sharp
            slopes = dot_t(pair, block[:, : 2 * HEAD_DIM])
            pieces = []
            for j in range(4):
                piece = scores[:, j * rows : (j + 1) * rows]
                if first:
                    piece = jnp.where(lane + orders[j] * rows <= row, piece, FLOOR)
                else:
                    piece = piece + jnp.where(orders[j] <= own, 0.0, FLOOR)
                pieces.append(piece)
            high = jnp.maximum(
                jnp.maximum(pieces[0], pieces[1]), jnp.maximum(pieces[2], pieces[3])
            )
            high = jnp.broadcast_to(jnp.max(high, axis=1, keepdims=True), high.shape)
            if not first:
                old = top[g, span, :]
                high = jnp.maximum(old, high)
                shrink = jnp.exp2(old - high)
            top[g, span, :] = high
            weights, tilted = [], []
            for j in range(4):
                weights.append(jnp.exp2(pieces[j] - high))
                tilted.append(weights[j] * slopes[:, j * rows : (j + 1) * rows])
            tot_new = (weights[0] + weights[1]) + (weights[2] + weights[3])
            dri_new = (tilted[0] + tilted[1]) + (tilted[2] + tilted[3])
            low_w = jnp.concatenate([w.astype(jnp.bfloat16) for w in weights], axis=1)
            low_t = jnp.concatenate([t.astype(jnp.bfloat16) for t in tilted], axis=1)
            acc_new = dot_n(low_w, block[:, 2 * HEAD_DIM :])
            tan_new = dot_n(low_t, block[:, 2 * HEAD_DIM : 3 * HEAD_DIM])
            if first:
                tot[g, span, :] = tot_new
                dri[g, span, :] = dri_new
                acc[g, span, :] = acc_new
                tan[g, span, :] = tan_new
            else:
                tot[g, span, :] = tot[g, span, :] * shrink + tot_new
                dri[g, span, :] = dri[g, span, :] * shrink + dri_new
                tan[g, span, :] = tan[g, span, :] * shrink + tan_new
                acc[g, span, :] = (
                    acc[g, span, :] * jnp.concatenate([shrink, shrink], axis=1) + acc_new
                )
            return carry

        lax.fori_loop(0, stack // part_rows, part, 0)

    def turn(s, carry):
        @pl.when(jnp.logical_and(s >= groups, s < steps))
        def _():
            zs, g = source(s // groups), s % groups
            twin(zs, g).wait_recv()
            pass_on(zs, g)

        @pl.when(jnp.logical_and(s >= 1, s < steps + 1))
        def _():
            zs, g = source((s - 1) // groups), (s - 1) % groups
            twin_across(zs, g).wait_recv()
            twin_across(zs, g).start()

        def ready(zs, g):
            move(zs, g, y, 1 - c, 0, at(z, y, 1 - c)).wait_recv()
            move(zs, g, 1 - y, 1 - c, 0, at(z, y, 1 - c)).wait_recv()

        @pl.when(jnp.logical_and(s >= 2, s < groups + 2))
        def _():
            g = s - 2
            ready(z, g)
            fold(z, g, True)

        @pl.when(s >= groups + 2)
        def _():
            zs, g = source((s - 2) // groups), (s - 2) % groups
            ready(zs, g)
            fold(zs, g, False)

        return carry

    lax.fori_loop(0, steps + 2, turn, 0)

    def finish(g, squares):
        for h in range(shares):
            span = slice(h * rows, (h + 1) * rows)
            cols = pl.ds(pl.multiple_of((g * shares + h) * HEAD_DIM, HEAD_DIM), HEAD_DIM)
            inverse = 1.0 / jnp.sum(tot[g, span, :], axis=1, keepdims=True)
            drift = jnp.sum(dri[g, span, :], axis=1, keepdims=True) * factor
            numer = acc[g, span, :HEAD_DIM] * inverse
            tangent = (tan[g, span, :] * factor + acc[g, span, HEAD_DIM:]) * inverse
            probe = tangent - numer * (drift * inverse)
            att_ref[:, cols] = numer.astype(jnp.bfloat16)
            probe_ref[:, cols] = probe.astype(jnp.bfloat16)
            squares = squares + jnp.sum((probe * probe).reshape(rows // 8, 8, HEAD_DIM), axis=0)
        return squares

    squares = lax.fori_loop(0, groups, finish, jnp.zeros((8, HEAD_DIM), jnp.float32))

    def add_up(value, box, sem, partners):
        count, mine, device = partners
        box[mine] = value

        def pass_to(step, slot):
            return pltpu.make_async_remote_copy(
                src_ref=box.at[mine],
                dst_ref=box.at[slot],
                send_sem=sem.at[0, step],
                recv_sem=sem.at[1, slot],
                device_id=device((mine + step) % count),
                device_id_type=MESH,
            )

        for step in range(1, count):
            pass_to(step, mine).start()
        for step in range(1, count):
            pass_to(step, (mine + step) % count).wait_recv()
        for step in range(1, count):
            pass_to(step, mine).wait_send()
        return jnp.sum(box[...], axis=0)

    squares = add_up(squares, plane_box, plane_sem, plane)
    squares = add_up(squares, line_box, line_sem, line)
    if heads > 1:
        squares = add_up(squares, head_box, head_sem, across_heads)
    entries = rows * q_vm.shape[1] * n * heads
    total = jnp.sum(jnp.sum(squares, axis=0, keepdims=True), axis=1, keepdims=True)
    norm_ref[...] = jnp.sqrt(total / entries)

    def settle(s, carry):
        zs, g = s // groups, s % groups

        @pl.when(goes_up(zs))
        def _():
            up(zs, g).wait_send()

        @pl.when(goes_down(zs))
        def _():
            down(zs, g).wait_send()

        across(zs, g).wait_send()
        twin(zs, g).wait_send()
        twin_across(zs, g).wait_send()
        return carry

    lax.fori_loop(0, steps, settle, 0)


def shards(n, heads, queries, key_rows, value_rows, query_tangent, key_tangent, value_tangent, block_order):
    rows, width = queries.shape
    groups = key_rows.shape[1] // HEAD_DIM
    stack = rows * width // key_rows.shape[1]
    depth = n // 4
    vmem = pl.BlockSpec(memory_space=pltpu.VMEM)
    hbm = pl.BlockSpec(memory_space=pl.ANY)
    f32, bf16 = jnp.float32, jnp.bfloat16
    attended, probe_out, norm = pl.pallas_call(
        functools.partial(kernel, n, heads),
        out_shape=(
            jax.ShapeDtypeStruct((rows, width), bf16),
            jax.ShapeDtypeStruct((rows, width), bf16),
            jax.ShapeDtypeStruct((1, 1), f32),
        ),
        in_specs=[pl.BlockSpec(memory_space=pltpu.SMEM), hbm, hbm, vmem, vmem, vmem, vmem],
        out_specs=(vmem, vmem, vmem),
        scratch_shapes=[
            pltpu.VMEM((rows, width), bf16),
            pltpu.VMEM((rows, width), bf16),
            pltpu.VMEM((groups, stack, 2 * HEAD_DIM), bf16),
            pltpu.VMEM((depth, groups, 2, 2, rows, 4 * HEAD_DIM), bf16),
            pltpu.VMEM((groups, stack, 2 * HEAD_DIM), f32),
            pltpu.VMEM((groups, stack, HEAD_DIM), f32),
            pltpu.VMEM((groups, stack, HEAD_DIM), f32),
            pltpu.VMEM((groups, stack, HEAD_DIM), f32),
            pltpu.VMEM((groups, stack, HEAD_DIM), f32),
            pltpu.VMEM((4, 8, HEAD_DIM), f32),
            pltpu.VMEM((depth, 8, HEAD_DIM), f32),
            pltpu.VMEM((heads, 8, HEAD_DIM), f32),
            pltpu.SemaphoreType.DMA((2,)),
            pltpu.SemaphoreType.DMA((depth, groups, 2, 2)),
            pltpu.SemaphoreType.DMA((depth, groups, 5)),
            pltpu.SemaphoreType.DMA((2, 4)),
            pltpu.SemaphoreType.DMA((2, depth)),
            pltpu.SemaphoreType.DMA((2, heads)),
        ],
        compiler_params=pltpu.CompilerParams(
            collective_id=0, has_side_effects=True, vmem_limit_bytes=56 * 2**20
        ),
    )(block_order, queries, query_tangent, key_rows, value_rows, key_tangent, value_tangent)
    return attended, probe_out, norm.reshape(())


def solution(mesh):
    split = P("ctx", "head")
    return jax.shard_map(
        functools.partial(shards, mesh.shape["ctx"], mesh.shape["head"]),
        mesh=mesh,
        in_specs=(split,) * 6 + (P(),),
        out_specs=(split, split, P()),
        check_vma=False,
    )
```

```python
import functools
import math

import jax
import jax.numpy as jnp
from jax import lax
from jax.experimental import pallas as pl
from jax.experimental.pallas import tpu as pltpu
from jax.sharding import PartitionSpec as P

HEAD_DIM = 128
MESH = pl.DeviceIdType.MESH
FLOOR = -1e30


def dot_t(a, b):
    return lax.dot_general(a, b, (((1,), (1,)), ((), ())), preferred_element_type=jnp.float32)


def dot_n(a, b):
    return jnp.dot(a, b, preferred_element_type=jnp.float32)


def kernel(
    n,
    heads,
    order_ref, q_hbm, dq_hbm, k_ref, v_ref, dk_ref, dv_ref,
    att_ref, probe_ref, norm_ref,
    q_vm, dq_vm, qs, kv, acc, tan, top, tot, dri,
    plane_box, line_box, head_box,
    q_sem, recv, send, plane_sem, line_sem, head_sem,
):
    depth = n // 4
    me = lax.axis_index("ctx")
    z, y, c = me // 4, (me // 2) % 2, me % 2
    rows = k_ref.shape[0]
    groups = k_ref.shape[1] // HEAD_DIM
    shares = q_vm.shape[1] // k_ref.shape[1]
    stack = rows * shares
    steps = depth * groups

    def at(zz, yy, cc):
        return {"ctx": (zz * 2 + yy) * 2 + cc}

    copies = [
        pltpu.make_async_copy(q_hbm, q_vm, q_sem.at[0]),
        pltpu.make_async_copy(dq_hbm, dq_vm, q_sem.at[1]),
    ]
    for copy in copies:
        copy.start()

    barrier = pltpu.get_barrier_semaphore()
    has_up, has_down = z < depth - 1, z > 0

    head = lax.axis_index("head")
    spot = y * 2 + c
    plane = (4, spot, lambda i: {"ctx": z * 4 + i})
    line = (depth, z, lambda i: {"ctx": i * 4 + spot})
    across_heads = (heads, head, lambda i: {"head": i})
    for count, mine, device in (plane, line, across_heads):
        for step in range(1, count):
            pl.semaphore_signal(
                barrier, inc=1, device_id=device((mine + step) % count), device_id_type=MESH
            )

    for g in range(groups):
        cols = slice(g * HEAD_DIM, (g + 1) * HEAD_DIM)
        for part, ref in enumerate((k_ref, dk_ref, v_ref, dv_ref)):
            kv[z, g, y, c, :, part * HEAD_DIM : (part + 1) * HEAD_DIM] = ref[:, cols]

    pl.semaphore_wait(barrier, 3 + (depth - 1) + (heads - 1))

    def move(zs, g, yy, cc, lane, target):
        return pltpu.make_async_remote_copy(
            src_ref=kv.at[zs, g, yy, cc],
            dst_ref=kv.at[zs, g, yy, cc],
            send_sem=send.at[zs, g, lane],
            recv_sem=recv.at[zs, g, yy, cc],
            device_id=target,
            device_id_type=MESH,
        )

    def up(zs, g):
        return move(zs, g, y, c, 0, at(z + 1, y, c))

    def down(zs, g):
        return move(zs, g, y, c, 1, at(z - 1, y, c))

    def across(zs, g):
        return move(zs, g, y, c, 2, at(z, 1 - y, c))

    def twin(zs, g):
        return move(zs, g, y, c, 3, at(z, y, 1 - c))

    def twin_across(zs, g):
        return move(zs, g, 1 - y, c, 4, at(z, y, 1 - c))

    def goes_up(zs):
        return jnp.logical_and(has_up, zs <= z)

    def goes_down(zs):
        return jnp.logical_and(has_down, zs >= z)

    def pass_on(zs, g):
        @pl.when(goes_up(zs))
        def _():
            up(zs, g).start()

        @pl.when(goes_down(zs))
        def _():
            down(zs, g).start()

        across(zs, g).start()
        twin(zs, g).start()

    for g in range(groups):
        pass_on(z, g)

    for copy in copies:
        copy.wait()

    def stage(g, carry):
        for h in range(shares):
            cols = pl.ds(pl.multiple_of((g * shares + h) * HEAD_DIM, HEAD_DIM), HEAD_DIM)
            qs[g, h * rows : (h + 1) * rows, 0:HEAD_DIM] = dq_vm[:, cols]
            qs[g, h * rows : (h + 1) * rows, HEAD_DIM:] = q_vm[:, cols]
        return carry

    lax.fori_loop(0, groups, stage, 0)

    reach = jnp.minimum(z, depth - 1 - z)
    far = jnp.where(z < depth - 1 - z, 1, -1)

    def source(i):
        near = ((i + 1) // 2) * jnp.where(i % 2 == 1, 1, -1)
        return z + jnp.where(i <= 2 * reach, near, (i - reach) * far)

    own = order_ref[me]
    factor = 1.0 / math.sqrt(HEAD_DIM)
    sharp = factor * math.log2(math.e)
    part_rows = min(stack, 1024)

    def fold(zs, g, first):
        block = kv[zs, g].reshape(4 * rows, 4 * HEAD_DIM)
        orders = [order_ref[zs * 4 + j] for j in range(4)]
        if first:
            lane = lax.broadcasted_iota(jnp.int32, (part_rows, rows), 1)
            row = lax.broadcasted_iota(jnp.int32, (part_rows, rows), 0) % rows + own * rows

        def part(r, carry):
            span = pl.ds(pl.multiple_of(r * part_rows, part_rows), part_rows)
            pair = qs[g, span, :]
            scores = dot_t(pair[:, HEAD_DIM:], block[:, :HEAD_DIM]) * sharp
            slopes = dot_t(pair, block[:, : 2 * HEAD_DIM])
            pieces = []
            for j in range(4):
                piece = scores[:, j * rows : (j + 1) * rows]
                if first:
                    piece = jnp.where(lane + orders[j] * rows <= row, piece, FLOOR)
                else:
                    piece = piece + jnp.where(orders[j] <= own, 0.0, FLOOR)
                pieces.append(piece)
            high = jnp.maximum(
                jnp.maximum(pieces[0], pieces[1]), jnp.maximum(pieces[2], pieces[3])
            )
            high = jnp.broadcast_to(jnp.max(high, axis=1, keepdims=True), high.shape)
            if not first:
                old = top[g, span, :]
                high = jnp.maximum(old, high)
                shrink = jnp.exp2(old - high)
            top[g, span, :] = high
            weights, tilted = [], []
            for j in range(4):
                weights.append(jnp.exp2(pieces[j] - high))
                tilted.append(weights[j] * slopes[:, j * rows : (j + 1) * rows])
            tot_new = (weights[0] + weights[1]) + (weights[2] + weights[3])
            dri_new = (tilted[0] + tilted[1]) + (tilted[2] + tilted[3])
            low_w = jnp.concatenate([w.astype(jnp.bfloat16) for w in weights], axis=1)
            low_t = jnp.concatenate([t.astype(jnp.bfloat16) for t in tilted], axis=1)
            acc_new = dot_n(low_w, block[:, 2 * HEAD_DIM :])
            tan_new = dot_n(low_t, block[:, 2 * HEAD_DIM : 3 * HEAD_DIM])
            if first:
                tot[g, span, :] = tot_new
                dri[g, span, :] = dri_new
                acc[g, span, :] = acc_new
                tan[g, span, :] = tan_new
            else:
                tot[g, span, :] = tot[g, span, :] * shrink + tot_new
                dri[g, span, :] = dri[g, span, :] * shrink + dri_new
                tan[g, span, :] = tan[g, span, :] * shrink + tan_new
                acc[g, span, :] = (
                    acc[g, span, :] * jnp.concatenate([shrink, shrink], axis=1) + acc_new
                )
            return carry

        lax.fori_loop(0, stack // part_rows, part, 0)

    def turn(s, carry):
        @pl.when(jnp.logical_and(s >= groups, s < steps))
        def _():
            zs, g = source(s // groups), s % groups
            twin(zs, g).wait_recv()
            pass_on(zs, g)

        @pl.when(jnp.logical_and(s >= 2, s < steps + 2))
        def _():
            zs, g = source((s - 2) // groups), (s - 2) % groups
            twin_across(zs, g).wait_recv()
            twin_across(zs, g).start()

        def ready(zs, g):
            move(zs, g, y, 1 - c, 0, at(z, y, 1 - c)).wait_recv()
            move(zs, g, 1 - y, 1 - c, 0, at(z, y, 1 - c)).wait_recv()

        @pl.when(jnp.logical_and(s >= 3, s < groups + 3))
        def _():
            g = s - 3
            ready(z, g)
            fold(z, g, True)

        @pl.when(s >= groups + 3)
        def _():
            zs, g = source((s - 3) // groups), (s - 3) % groups
            ready(zs, g)
            fold(zs, g, False)

        return carry

    lax.fori_loop(0, steps + 3, turn, 0)

    def finish(g, squares):
        for h in range(shares):
            span = slice(h * rows, (h + 1) * rows)
            cols = pl.ds(pl.multiple_of((g * shares + h) * HEAD_DIM, HEAD_DIM), HEAD_DIM)
            inverse = 1.0 / jnp.sum(tot[g, span, :], axis=1, keepdims=True)
            drift = jnp.sum(dri[g, span, :], axis=1, keepdims=True) * factor
            numer = acc[g, span, :HEAD_DIM] * inverse
            tangent = (tan[g, span, :] * factor + acc[g, span, HEAD_DIM:]) * inverse
            probe = tangent - numer * (drift * inverse)
            att_ref[:, cols] = numer.astype(jnp.bfloat16)
            probe_ref[:, cols] = probe.astype(jnp.bfloat16)
            squares = squares + jnp.sum((probe * probe).reshape(rows // 8, 8, HEAD_DIM), axis=0)
        return squares

    squares = lax.fori_loop(0, groups, finish, jnp.zeros((8, HEAD_DIM), jnp.float32))

    def add_up(value, box, sem, partners):
        count, mine, device = partners
        box[mine] = value

        def pass_to(step, slot):
            return pltpu.make_async_remote_copy(
                src_ref=box.at[mine],
                dst_ref=box.at[slot],
                send_sem=sem.at[0, step],
                recv_sem=sem.at[1, slot],
                device_id=device((mine + step) % count),
                device_id_type=MESH,
            )

        for step in range(1, count):
            pass_to(step, mine).start()
        for step in range(1, count):
            pass_to(step, (mine + step) % count).wait_recv()
        for step in range(1, count):
            pass_to(step, mine).wait_send()
        return jnp.sum(box[...], axis=0)

    squares = add_up(squares, plane_box, plane_sem, plane)
    squares = add_up(squares, line_box, line_sem, line)
    if heads > 1:
        squares = add_up(squares, head_box, head_sem, across_heads)
    entries = rows * q_vm.shape[1] * n * heads
    total = jnp.sum(jnp.sum(squares, axis=0, keepdims=True), axis=1, keepdims=True)
    norm_ref[...] = jnp.sqrt(total / entries)

    def settle(s, carry):
        zs, g = s // groups, s % groups

        @pl.when(goes_up(zs))
        def _():
            up(zs, g).wait_send()

        @pl.when(goes_down(zs))
        def _():
            down(zs, g).wait_send()

        across(zs, g).wait_send()
        twin(zs, g).wait_send()
        twin_across(zs, g).wait_send()
        return carry

    lax.fori_loop(0, steps, settle, 0)


def shards(n, heads, queries, key_rows, value_rows, query_tangent, key_tangent, value_tangent, block_order):
    rows, width = queries.shape
    groups = key_rows.shape[1] // HEAD_DIM
    stack = rows * width // key_rows.shape[1]
    depth = n // 4
    vmem = pl.BlockSpec(memory_space=pltpu.VMEM)
    hbm = pl.BlockSpec(memory_space=pl.ANY)
    f32, bf16 = jnp.float32, jnp.bfloat16
    attended, probe_out, norm = pl.pallas_call(
        functools.partial(kernel, n, heads),
        out_shape=(
            jax.ShapeDtypeStruct((rows, width), bf16),
            jax.ShapeDtypeStruct((rows, width), bf16),
            jax.ShapeDtypeStruct((1, 1), f32),
        ),
        in_specs=[pl.BlockSpec(memory_space=pltpu.SMEM), hbm, hbm, vmem, vmem, vmem, vmem],
        out_specs=(vmem, vmem, vmem),
        scratch_shapes=[
            pltpu.VMEM((rows, width), bf16),
            pltpu.VMEM((rows, width), bf16),
            pltpu.VMEM((groups, stack, 2 * HEAD_DIM), bf16),
            pltpu.VMEM((depth, groups, 2, 2, rows, 4 * HEAD_DIM), bf16),
            pltpu.VMEM((groups, stack, 2 * HEAD_DIM), f32),
            pltpu.VMEM((groups, stack, HEAD_DIM), f32),
            pltpu.VMEM((groups, stack, HEAD_DIM), f32),
            pltpu.VMEM((groups, stack, HEAD_DIM), f32),
            pltpu.VMEM((groups, stack, HEAD_DIM), f32),
            pltpu.VMEM((4, 8, HEAD_DIM), f32),
            pltpu.VMEM((depth, 8, HEAD_DIM), f32),
            pltpu.VMEM((heads, 8, HEAD_DIM), f32),
            pltpu.SemaphoreType.DMA((2,)),
            pltpu.SemaphoreType.DMA((depth, groups, 2, 2)),
            pltpu.SemaphoreType.DMA((depth, groups, 5)),
            pltpu.SemaphoreType.DMA((2, 4)),
            pltpu.SemaphoreType.DMA((2, depth)),
            pltpu.SemaphoreType.DMA((2, heads)),
        ],
        compiler_params=pltpu.CompilerParams(
            collective_id=0, has_side_effects=True, vmem_limit_bytes=56 * 2**20
        ),
    )(block_order, queries, query_tangent, key_rows, value_rows, key_tangent, value_tangent)
    return attended, probe_out, norm.reshape(())


def solution(mesh):
    split = P("ctx", "head")
    return jax.shard_map(
        functools.partial(shards, mesh.shape["ctx"], mesh.shape["head"]),
        mesh=mesh,
        in_specs=(split,) * 6 + (P(),),
        out_specs=(split, split, P()),
        check_vma=False,
    )
```
